128 devices in a mesh: prow: 8 (over x, core), pcol: 16 (over z, y).
Axes of the slice: x: 4, y: 4, z: 4, core: 2. Of those that a mesh axis runs over, the one named last changes fastest.
Arguments:
- l_panel: float32 [256, 256], replicated, may hold values from -0.5 to 3, as said below
- l_rows: float32 [8, 256, 12, 256], P('prow', 'pcol'), may hold values from -0.0390625 to 0.0390625
- lbar_panel: float32 [256, 256], replicated, may hold values from -6 to 6
- lbar_rows: float32 [8, 256, 12, 256], P('prow', 'pcol'), may hold values from -6 to 6
- sbar: float32 [8, 256, 12, 16, 6, 256], P('prow', None, None, 'pcol'), may hold values from -90 to 90, as said below
Outputs:
- abar_rows: float32 [8, 256, 12, 256], P('prow', 'pcol')
- abar_panel: float32 [256, 256], replicated
The draws below stay inside these ranges and needn't reach their ends.
Inputs may be any that keep to these rules, and one draw needn't show every extreme that they name: `l_panel`: lower triangular; diagonal entries between 2 and 3. `sbar`: S read from it is symmetric.
All inputs are finite; a program needn't handle non-finite values.
Results may differ from the reference program's by a relative error of at most 0.000068.
Values sent between devices are 32-bit elements; how exact they have to be, the bound alone decides.
No kernel may reach another device: no remote copies, remote signals or barrier semaphores. Data moves between devices by JAX's collectives and lax.ppermute only.
A program may use at most 192 MiB of HBM per device.

```python
import jax
import jax.numpy as jnp
from jax import lax

NB = 256
TPC = 6
UR = 12
M = 24576
N_PROW = 8
N_PCOL = 16


def draw_l_panel(key, part):
    key = jax.random.fold_in(key, 7)
    key_diag, key_off = jax.random.split(key)
    diag_vals = jax.random.uniform(key_diag, (NB,), jnp.float32, 2.0, 3.0)
    off = jax.random.normal(key_off, (NB, NB), jnp.float32) / NB ** 0.5
    off = jnp.clip(off, -0.5, 0.5)
    rows = lax_rows(NB)
    lower = (rows[:, None] > rows[None, :]).astype(jnp.float32)
    return off * lower + jnp.diag(diag_vals)


def lax_rows(count):
    return jnp.arange(count, dtype=jnp.int32)


def draw_sbar(key, part):
    key = jax.random.fold_in(key, 11)
    key_base = jax.random.fold_in(key, 0)
    base = jnp.clip(jax.random.normal(key_base, (M, M), jnp.float32), -6.0, 6.0)
    sym = (base + base.T) * 0.70710678
    return jnp.transpose(sym.reshape(UR, N_PROW, NB, TPC, N_PCOL, NB), (1, 2, 0, 4, 3, 5))


def level_of(stream_key, dims, cuts, smallest, largest):
    def one(dim, blocks):
        steps = jax.random.uniform(jax.random.fold_in(jax.random.fold_in(stream_key, 6), dim), (blocks,), jnp.float32, smallest / len(cuts), largest / len(cuts))
        return jnp.repeat(jnp.exp(steps), dims[dim] // blocks).reshape((-1,) + (1,) * (len(dims) - dim - 1))

    factor_of = one(*cuts[0])
    for cut in cuts[1:]:
        factor_of = factor_of * one(*cut)
    return factor_of


def scatter_about(rng, extent, scale, most, shards=(), kind=jnp.bfloat16):
    result = jax.random.normal(rng, extent, jnp.float32) * scale
    if len(shards) > 0:
        result = level_of(rng, extent, shards, -0.22, 0.18) * result
    return jnp.clip(result, min=-most, max=most).astype(kind)


def setup_inputs(seed: int = 0) -> dict:
    arg_keys = jax.random.split(jax.random.key(seed), 6)
    l_panel = draw_l_panel(jax.random.fold_in(arg_keys[5], 71), 0)
    l_rows = scatter_about(arg_keys[1], (N_PROW, NB, UR, NB), M ** -0.5, 0.0390625, ((0, 8), (1, 16)), jnp.float32)
    lbar_panel = scatter_about(arg_keys[2], (NB, NB), 1.0, 6.0, (), jnp.float32)
    lbar_rows = scatter_about(arg_keys[3], (N_PROW, NB, UR, NB), 1.0, 6.0, ((0, 8), (1, 16)), jnp.float32)
    sbar = draw_sbar(jax.random.fold_in(arg_keys[5], 71), 0)
    return {"l_panel": l_panel, "l_rows": l_rows, "lbar_panel": lbar_panel, "lbar_rows": lbar_rows, "sbar": sbar}


def hdot(left, right):
    return jnp.dot(left.astype(jnp.float32), right.astype(jnp.float32), precision=lax.Precision.HIGHEST, preferred_element_type=jnp.float32)

def reference(l_panel, l_rows, lbar_panel, lbar_rows, sbar):
    width = l_rows.shape[3]
    factor_rows = jnp.transpose(l_rows, (2, 0, 1, 3)).reshape(M, width)
    adjoint_rows = jnp.transpose(lbar_rows, (2, 0, 1, 3)).reshape(M, width)
    matrix = jnp.transpose(sbar, (2, 0, 1, 4, 3, 5)).reshape(M, M)
    identity = jnp.eye(width, dtype=l_panel.dtype)
    inverse = lax.linalg.triangular_solve(l_panel, identity, left_side=True, lower=True)
    product = hdot(matrix, factor_rows)
    adjusted = adjoint_rows - 2.0 * product
    abar_full = hdot(adjusted, inverse)
    gram = hdot(abar_full.T, factor_rows)
    lbar_new = lbar_panel - jnp.tril(gram)
    inner = hdot(l_panel.T, lbar_new)
    phi = jnp.tril(inner) - 0.5 * jnp.diag(jnp.diag(inner))
    qmat = hdot(hdot(inverse.T, phi), inverse)
    abar_panel = 0.5 * (qmat + qmat.T)
    abar_rows = jnp.transpose(abar_full.reshape(UR, N_PROW, NB, width), (1, 2, 0, 3))
    return (abar_rows, abar_panel)
```

```python
import functools

import jax
import jax.numpy as jnp
from jax import lax
from jax.experimental import pallas as pl
from jax.experimental.pallas import tpu as pltpu
from jax.sharding import PartitionSpec as P

F32 = jnp.float32
BF16 = jnp.bfloat16
AXES = ("prow", "pcol")
NB = 256
UR = 12
TPC = 6
PIECE = 16 * UR
GROUP = 4 * PIECE
SLAB = PIECE * TPC * 2
COLS = TPC * NB
VMEM = pl.BlockSpec(memory_space=pltpu.VMEM)
ANY = pl.BlockSpec(memory_space=pl.ANY)


def pairs(target):
    found = []
    for x in range(4):
        for c in range(2):
            for z in range(4):
                for y in range(4):
                    tx, tc, tz, ty = target(x, c, z, y)
                    found.append(
                        ((2 * x + c) * 16 + 4 * z + y, (2 * (tx % 4) + tc) * 16 + 4 * (tz % 4) + ty % 4)
                    )
    return found


def permute(value, target):
    return lax.ppermute(value, AXES, pairs(target))


def first_axis(step):
    return lambda x, c, z, y: (x, c, z, y + step) if c == 0 else (x, c, z + step, y)


def second_axis(step):
    return lambda x, c, z, y: (x, c, z + step, y) if c == 0 else (x, c, z, y + step)


def other_core(x, c, z, y):
    return x, 1 - c, z, y


def halving(stage):
    def target(x, c, z, y):
        return (x ^ 1 if (stage + c) % 2 == 0 else x ^ 3), c, z, y

    return target


def crossing(stage, mask):
    def target(x, c, z, y):
        axis = (stage + c) % 3
        if axis == 0:
            return x ^ mask, c, z, y
        if axis == 1:
            return x, c, z, y ^ mask
        return x, c, z ^ mask, y

    return target


def to_tiles(k):
    def target(x, c, z, y):
        p, q = 2 * x + c, 4 * z + y
        parity = k ^ (q % 2)
        tp, tq = q // 2, p + 8 * parity
        return tp // 2, tp % 2, tq // 4, tq % 4

    return target


def to_rows(k):
    def target(x, c, z, y):
        p, q = 2 * x + c, 4 * z + y
        half = k ^ (q // 8)
        tp, tq = q % 8, 2 * p + half
        return tp // 2, tp % 2, tq // 4, tq % 4

    return target


def place():
    p, q = lax.axis_index("prow"), lax.axis_index("pcol")
    return p // 2, p % 2, q // 4, q % 4


def split(value):
    high = value.astype(BF16)
    return high, (value - high.astype(F32)).astype(BF16)


def dot3(lh, ll, rh, rl):
    total = jnp.dot(lh, rh, preferred_element_type=F32)
    total += jnp.dot(ll, rh, preferred_element_type=F32)
    total += jnp.dot(lh, rl, preferred_element_type=F32)
    return total


def dot6(left, right):
    return jnp.dot(left, right, precision=lax.Precision.HIGHEST, preferred_element_type=F32)


def tdot6(left, right):
    return lax.dot_general(
        left, right, (((0,), (0,)), ((), ())), precision=lax.Precision.HIGHEST, preferred_element_type=F32
    )


def prep_kernel(step, s_ref, high_ref, low_ref, buffer, sem):
    _, c, z, y = place()
    copies = []
    for i, offset in enumerate((0, 3, 1, 2)):
        zz = jnp.where(c == 0, z + step, z + offset) % 4
        yy = jnp.where(c == 0, y + offset, y + step) % 4
        base = (zz * 4 + yy) * SLAB
        for j in range(2):
            half = SLAB // 2
            copy = pltpu.make_async_copy(
                s_ref.at[pl.ds(base + j * half, half), :],
                buffer.at[pl.ds(i * SLAB + j * half, half), :],
                sem.at[2 * i + j],
            )
            copy.start()
            copies.append(copy)
    rows = PIECE // 2
    for i, copy in enumerate(copies):
        copy.wait()
        for k in range(2 * TPC):
            high, low = split(buffer[pl.ds(i * (SLAB // 2) + k, rows, stride=2 * TPC), :])
            high_ref[i * rows : (i + 1) * rows, k * 128 : (k + 1) * 128] = high
            low_ref[i * rows : (i + 1) * rows, k * 128 : (k + 1) * 128] = low


def prepare(step, s_lines):
    return pl.pallas_call(
        functools.partial(prep_kernel, step),
        in_specs=[ANY],
        out_specs=[VMEM, VMEM],
        out_shape=[jax.ShapeDtypeStruct((GROUP, COLS), BF16)] * 2,
        scratch_shapes=[pltpu.VMEM((4 * SLAB, 128), F32), pltpu.SemaphoreType.DMA((8,))],
        compiler_params=pltpu.CompilerParams(vmem_limit_bytes=40 << 20),
        cost_estimate=pl.CostEstimate(flops=0, bytes_accessed=10_000_000, transcendentals=0),
        name="prepare",
    )(s_lines)


def multiply_kernel(count, *refs):
    groups, out_ref = refs[:-1], refs[-1]
    total = None
    for i in range(count):
        l_ref, high_ref, low_ref = groups[3 * i : 3 * i + 3]
        lh, ll = split(l_ref[...].T)
        part = dot3(lh, ll, high_ref[...], low_ref[...])
        total = part if total is None else total + part
    if len(groups) > 3 * count:
        total += groups[-1][...]
    out_ref[...] = total


def multiply(*operands):
    count = len(operands) // 3
    return pl.pallas_call(
        functools.partial(multiply_kernel, count),
        in_specs=[VMEM] * len(operands),
        out_specs=VMEM,
        out_shape=jax.ShapeDtypeStruct((NB, COLS), F32),
        compiler_params=pltpu.CompilerParams(vmem_limit_bytes=48 << 20),
        cost_estimate=pl.CostEstimate(
            flops=count * 6 * GROUP * COLS * NB, bytes_accessed=count * 6_000_000, transcendentals=0
        ),
        name="multiply",
    )(*operands)


def finish_kernel(la_ref, lb_ref, high_ref, low_ref, acc_ref, cols_ref, keep_ref, send_ref, cross_ref):
    x, c, _, _ = place()
    lh, ll = split(jnp.concatenate([la_ref[...], lb_ref[...]], axis=0).T)
    cross = None
    for half in range(3):
        at = slice(half * 512, (half + 1) * 512)
        part = acc_ref[:, at] + dot3(lh, ll, high_ref[:, at], low_ref[:, at])
        turned = part.T
        for j in range(2):
            v = 2 * half + j
            block = turned[j * NB : (j + 1) * NB].reshape(8, 32, NB)
            rows = cols_ref[:, v].reshape(NB, NB)
            for xx in range(4):
                for core in range(2):
                    piece = block[2 * xx + core]
                    away = xx ^ x
                    if core == 0:
                        order = jnp.where(away == 0, 0, jnp.where(away == 3, 1, jnp.where(away == 1, 2, 3)))
                    else:
                        order = jnp.where(away == 0, 0, jnp.where(away == 1, 1, jnp.where(away == 3, 2, 3)))

                    @pl.when(c == core)
                    def _():
                        keep_ref[order, v] = piece

                    @pl.when(c != core)
                    def _():
                        send_ref[order, v] = piece

            ph, pl_ = split(part[:, j * NB : (j + 1) * NB])
            rh, rl = split(rows)
            term = dot3(ph, pl_, rh, rl)
            cross = term if cross is None else cross + term
    cross_ref[...] = cross


def finish(la, lb, high, low, acc, cols):
    share = jax.ShapeDtypeStruct((4, TPC, 32, NB), F32)
    return pl.pallas_call(
        finish_kernel,
        in_specs=[VMEM] * 6,
        out_specs=[VMEM] * 3,
        out_shape=[share, share, jax.ShapeDtypeStruct((NB, NB), F32)],
        compiler_params=pltpu.CompilerParams(vmem_limit_bytes=48 << 20),
        cost_estimate=pl.CostEstimate(
            flops=7 * GROUP * COLS * NB, bytes_accessed=12_000_000, transcendentals=0
        ),
        name="finish",
    )(la, lb, high, low, acc, cols)


def invert_kernel(l_ref, out_ref):
    n = NB
    row = lax.broadcasted_iota(jnp.int32, (n, n), 0)
    col = lax.broadcasted_iota(jnp.int32, (n, n), 1)
    lower = l_ref[...]
    diagonal = jnp.where(row == col, lower, 0.0)
    by_row = 1.0 / jnp.sum(diagonal, axis=1, keepdims=True)
    by_col = 1.0 / jnp.sum(diagonal, axis=0, keepdims=True)
    strict = jnp.where(row > col, lower * by_row, 0.0)
    power = jnp.where(row // 16 == col // 16, -strict, 0.0)
    inverse = jnp.where(row == col, 1.0, 0.0) + power
    for _ in range(3):
        power = dot6(power, power)
        inverse = inverse + dot6(power, inverse)
    size = 16
    while size < n:
        beside = (row // (2 * size) == col // (2 * size)) & (row // size != col // size)
        inverse = inverse - dot6(inverse, dot6(jnp.where(beside, strict, 0.0), inverse))
        size *= 2
    out_ref[...] = inverse * by_col


def invert(l_panel):
    return pl.pallas_call(
        invert_kernel,
        in_specs=[VMEM],
        out_specs=VMEM,
        out_shape=jax.ShapeDtypeStruct((NB, NB), F32),
        compiler_params=pltpu.CompilerParams(vmem_limit_bytes=24 << 20),
        cost_estimate=pl.CostEstimate(flops=14 * 12 * NB**3, bytes_accessed=20_000_000, transcendentals=0),
        name="invert",
    )(l_panel)


def panel_kernel(share, cross_ref, own_ref, mine_ref, l_ref, inv_ref, lbar_ref, keep_ref, send_ref):
    _, c, _, _ = place()
    row = lax.broadcasted_iota(jnp.int32, (NB, NB), 0)
    col = lax.broadcasted_iota(jnp.int32, (NB, NB), 1)
    inverse = inv_ref[...]
    lower = l_ref[...]
    inner = tdot6(own_ref[...], mine_ref[...]) - 2.0 * cross_ref[...]
    gram = tdot6(inverse, inner)
    fresh = lbar_ref[...] * share - jnp.where(row >= col, gram, 0.0)
    phi = tdot6(lower, fresh)
    phi = jnp.where(row > col, phi, jnp.where(row == col, 0.5 * phi, 0.0))
    full = dot6(tdot6(inverse, phi), inverse)
    result = 0.5 * (full + full.T)
    first, second = result[: NB // 2], result[NB // 2 :]
    keep_ref[...] = jnp.where(c == 0, first, second)
    send_ref[...] = jnp.where(c == 0, second, first)


def panel(cross, own, mine, l_panel, inverse, lbar_panel, share):
    half = jax.ShapeDtypeStruct((NB // 2, NB), F32)
    return pl.pallas_call(
        functools.partial(panel_kernel, share),
        in_specs=[VMEM] * 6,
        out_specs=[VMEM] * 2,
        out_shape=[half, half],
        compiler_params=pltpu.CompilerParams(vmem_limit_bytes=24 << 20),
        cost_estimate=pl.CostEstimate(flops=5 * 12 * NB**3, bytes_accessed=8_000_000, transcendentals=0),
        name="panel",
    )(cross, own, mine, l_panel, inverse, lbar_panel)


def rows_kernel(own_ref, first_ref, second_ref, inv_ref, out_ref):
    _, _, _, y = place()
    swap = y % 2 == 1
    first, second = first_ref[...], second_ref[...]
    even = jnp.where(swap, second, first)
    odd = jnp.where(swap, first, second)
    adjusted = own_ref[...] - 2.0 * jnp.stack([even, odd], axis=1)
    result = dot6(adjusted.reshape(PIECE, NB), inv_ref[...])
    out_ref[...] = result.reshape(TPC, 2, 16, NB)


def finish_rows(own, first, second, inverse):
    return pl.pallas_call(
        rows_kernel,
        in_specs=[VMEM] * 4,
        out_specs=VMEM,
        out_shape=jax.ShapeDtypeStruct((TPC, 2, 16, NB), F32),
        compiler_params=pltpu.CompilerParams(vmem_limit_bytes=24 << 20),
        cost_estimate=pl.CostEstimate(flops=12 * PIECE * NB * NB, bytes_accessed=1_000_000, transcendentals=0),
        name="finish_rows",
    )(own, first, second, inverse)


def shards(l_panel, l_rows, lbar_panel, lbar_rows, sbar):
    p, q = lax.axis_index("prow"), lax.axis_index("pcol")
    s_lines = sbar.reshape(16 * SLAB, 128)
    by_tile = jnp.transpose(l_rows[0], (1, 0, 2))
    own = jnp.transpose(lbar_rows[0], (1, 0, 2))
    piece = l_rows[0].reshape(PIECE, NB)

    tiles = by_tile.reshape(TPC, 2, 16, NB)
    odd_col = q % 2 == 1
    even_u, odd_u = tiles[:, 0], tiles[:, 1]
    t0 = permute(jnp.where(odd_col, odd_u, even_u), to_tiles(0))
    t1 = permute(jnp.where(odd_col, even_u, odd_u), to_tiles(1))
    late = q >= 8
    col_piece = jnp.concatenate([jnp.where(late, t1, t0), jnp.where(late, t0, t1)], axis=1)
    cols = lax.all_gather(col_piece, "prow", axis=0, tiled=False)

    up = permute(piece, first_axis(1))
    down = permute(piece, first_axis(-1))
    far_up = permute(up[: PIECE // 2], first_axis(1))
    far_down = permute(down[PIECE // 2 :], first_axis(-1))
    group = jnp.concatenate([piece, up, down, far_up, far_down], axis=0)
    group_up = permute(group, second_axis(1))
    group_down = permute(group, second_axis(-1))
    group_far_up = permute(group_up[: GROUP // 2], second_axis(1))
    group_far_down = permute(group_down[GROUP // 2 :], second_axis(-1))

    parts = [prepare(step, s_lines) for step in (0, 3, 1, 2)]
    inverse = invert(l_panel)
    total = multiply(group, *parts[0])
    total = multiply(group_up, *parts[1], group_down, *parts[2], total)
    keep, send, cross = finish(group_far_up, group_far_down, *parts[3], total, cols)

    keep = keep + permute(send, other_core)
    keep = keep[:2] + permute(keep[2:], halving(0))
    product = keep[0] + permute(keep[1], halving(1))
    product = product.reshape(TPC, 2, 16, NB)
    r0 = permute(jnp.where(late, product[:, 1], product[:, 0]), to_rows(0))
    r1 = permute(jnp.where(late, product[:, 0], product[:, 1]), to_rows(1))
    abar = finish_rows(own.reshape(TPC, 2, 16, NB), r0, r1, inverse)
    abar_rows = jnp.transpose(abar.reshape(UR, 16, NB), (1, 0, 2))[None]

    share = 1.0 / (lax.axis_size("prow") * lax.axis_size("pcol"))
    mine = by_tile.reshape(PIECE, NB)
    part, other = panel(cross, own.reshape(PIECE, NB), mine, l_panel, inverse, lbar_panel, share)
    part = part + permute(other, other_core)
    for stage in range(3):
        near, opposite, beyond = (permute(part, crossing(stage, mask)) for mask in (1, 3, 2))
        part = (part + near) + (beyond + opposite)
    rest = permute(part, other_core)
    is_first = p % 2 == 0
    abar_panel = jnp.concatenate([jnp.where(is_first, part, rest), jnp.where(is_first, rest, part)], axis=0)
    return abar_rows, abar_panel


def solution(mesh):
    return jax.shard_map(
        shards,
        mesh=mesh,
        in_specs=(
            P(),
            P("prow", "pcol", None, None),
            P(),
            P("prow", "pcol", None, None),
            P("prow", None, None, "pcol", None, None),
        ),
        out_specs=(P("prow", "pcol", None, None), P()),
        check_vma=False,
    )
```

```python
import functools

import jax
import jax.numpy as jnp
from jax import lax
from jax.experimental import pallas as pl
from jax.experimental.pallas import tpu as pltpu
from jax.sharding import PartitionSpec as P

F32 = jnp.float32
BF16 = jnp.bfloat16
AXES = ("prow", "pcol")
NB = 256
UR = 12
TPC = 6
PIECE = 16 * UR
GROUP = 4 * PIECE
SLAB = PIECE * TPC * 2
COLS = TPC * NB
VMEM = pl.BlockSpec(memory_space=pltpu.VMEM)
ANY = pl.BlockSpec(memory_space=pl.ANY)
HBM = pl.BlockSpec(memory_space=pltpu.HBM)


def pairs(target):
    found = []
    for x in range(4):
        for c in range(2):
            for z in range(4):
                for y in range(4):
                    tx, tc, tz, ty = target(x, c, z, y)
                    found.append(
                        ((2 * x + c) * 16 + 4 * z + y, (2 * (tx % 4) + tc) * 16 + 4 * (tz % 4) + ty % 4)
                    )
    return found


def permute(value, target):
    return lax.ppermute(value, AXES, pairs(target))


def first_axis(step):
    return lambda x, c, z, y: (x, c, z, y + step) if c == 0 else (x, c, z + step, y)


def second_axis(step):
    return lambda x, c, z, y: (x, c, z + step, y) if c == 0 else (x, c, z, y + step)


def other_core(x, c, z, y):
    return x, 1 - c, z, y


def halving(stage):
    def target(x, c, z, y):
        return (x ^ 1 if (stage + c) % 2 == 0 else x ^ 3), c, z, y

    return target


def crossing(stage, mask):
    def target(x, c, z, y):
        axis = (stage + c) % 3
        if axis == 0:
            return x ^ mask, c, z, y
        if axis == 1:
            return x, c, z, y ^ mask
        return x, c, z ^ mask, y

    return target


def opposite_half(x, c, z, y):
    return x, c, z ^ 2, y


def to_tiles(x, c, z, y):
    p, q = 2 * x + c, 4 * z + y
    tp, tq = (q % 8) ^ p, 8 * (q // 8) + p
    return tp // 2, tp % 2, tq // 4, tq % 4


def to_rows(x, c, z, y):
    p, q = 2 * x + c, 4 * z + y
    tp, tq = q % 8, 8 * (q // 8) + (p ^ (q % 8))
    return tp // 2, tp % 2, tq // 4, tq % 4


def place():
    p, q = lax.axis_index("prow"), lax.axis_index("pcol")
    return p // 2, p % 2, q // 4, q % 4


def split(value):
    high = value.astype(BF16)
    return high, (value - high.astype(F32)).astype(BF16)


def dot3(lh, ll, rh, rl):
    total = jnp.dot(lh, rh, preferred_element_type=F32)
    total += jnp.dot(ll, rh, preferred_element_type=F32)
    total += jnp.dot(lh, rl, preferred_element_type=F32)
    return total


def dot6(left, right):
    return jnp.dot(left, right, precision=lax.Precision.HIGHEST, preferred_element_type=F32)


def tdot6(left, right):
    return lax.dot_general(
        left, right, (((0,), (0,)), ((), ())), precision=lax.Precision.HIGHEST, preferred_element_type=F32
    )


def call(kernel, inputs, outputs, limit, flops=0, size=0, scratch=(), specs=None):
    if specs:
        inputs = [
            pltpu.with_memory_space_constraint(value, pltpu.HBM) if spec is HBM else value
            for value, spec in zip(inputs, specs)
        ]
    return pl.pallas_call(
        kernel,
        in_specs=specs or [VMEM] * len(inputs),
        out_specs=[VMEM] * len(outputs),
        out_shape=list(outputs),
        scratch_shapes=list(scratch),
        compiler_params=pltpu.CompilerParams(vmem_limit_bytes=limit << 20),
        cost_estimate=pl.CostEstimate(flops=flops, bytes_accessed=size, transcendentals=0),
        name=(kernel.func if isinstance(kernel, functools.partial) else kernel).__name__,
    )(*inputs)


def kept(*shape):
    return pltpu.VMEM(shape, F32)


def free(*shape):
    return jax.ShapeDtypeStruct(shape, F32)


def order_rows(l_ref, piece_ref):
    piece_ref[...] = jnp.swapaxes(l_ref[...], 0, 1).reshape(PIECE, NB)


def split_tiles(rows_ref, _, __, keep_ref, send_ref):
    high = place()[2] // 2
    for v in range(TPC):
        keep_ref[v] = rows_ref[2 * v + high]
        send_ref[v] = rows_ref[2 * v + 1 - high]


def join_group(own_ref, up_ref, down_ref, far_up_ref, far_down_ref, _, out_ref):
    out_ref[:PIECE] = own_ref[...]
    out_ref[PIECE : 2 * PIECE] = up_ref[...]
    out_ref[2 * PIECE : 3 * PIECE] = down_ref[...]
    out_ref[3 * PIECE : 3 * PIECE + PIECE // 2] = far_up_ref[...]
    out_ref[3 * PIECE + PIECE // 2 :] = far_down_ref[...]


def take_halves(up_ref, down_ref, _, __, first_ref, second_ref):
    first_ref[...] = up_ref[: GROUP // 2]
    second_ref[...] = down_ref[GROUP // 2 :]


def fetch(step, s_ref, held_ref, sem):
    _, c, z, y = place()
    copies = []
    for i, offset in enumerate((0, 3, 1, 2)):
        zz = jnp.where(c == 0, z + step, z + offset) % 4
        yy = jnp.where(c == 0, y + offset, y + step) % 4
        copy = pltpu.make_async_copy(
            s_ref.at[pl.ds((zz * 4 + yy) * SLAB, SLAB), :],
            held_ref.at[pl.ds(i * SLAB, SLAB), :],
            sem.at[i],
        )
        copy.start()
        copies.append(copy)
    return copies


def grids():
    row = lax.broadcasted_iota(jnp.int32, (NB, NB), 0)
    col = lax.broadcasted_iota(jnp.int32, (NB, NB), 1)
    return row, col


def invert_blocks(
    s_ref, l_ref, lbar_ref, own_ref, mine_ref, _, __,
    first_s, second_s, strict_ref, inverse_ref, l_out, lbar_out, own_out, mine_out, sem, small,
):
    panel = pltpu.make_async_copy(l_ref, l_out, small.at[0])
    panel.start()
    copies = fetch(0, s_ref, first_s, sem.at[0])
    for i, (src, dst) in enumerate(((lbar_ref, lbar_out), (own_ref, own_out), (mine_ref, mine_out))):
        copy = pltpu.make_async_copy(src, dst, small.at[i + 1])
        copy.start()
        copies.append(copy)
    copies += fetch(3, s_ref, second_s, sem.at[1])
    panel.wait()
    row, col = grids()
    lower = l_out[...]
    by_row = 1.0 / jnp.sum(jnp.where(row == col, lower, 0.0), axis=1, keepdims=True)
    strict = jnp.where(row > col, lower * by_row, 0.0)
    power = jnp.where(row // 16 == col // 16, -strict, 0.0)
    inverse = jnp.where(row == col, 1.0, 0.0) + power
    for _ in range(3):
        power = dot6(power, power)
        inverse = inverse + dot6(power, inverse)
    strict_ref[...] = strict
    inverse_ref[...] = inverse
    for copy in copies:
        copy.wait()


def invert_rest(s_ref, strict_ref, blocks_ref, l_ref, _, third_s, fourth_s, inverse_ref, sem):
    copies = fetch(1, s_ref, third_s, sem.at[0]) + fetch(2, s_ref, fourth_s, sem.at[1])

    @pl.when(place()[0] >= 0)
    def _():
        row, col = grids()
        strict = strict_ref[...]
        inverse = blocks_ref[...]
        size = 16
        while size < NB:
            beside = (row // (2 * size) == col // (2 * size)) & (row // size != col // size)
            inverse = inverse - dot6(inverse, dot6(jnp.where(beside, strict, 0.0), inverse))
            size *= 2
        by_col = 1.0 / jnp.sum(jnp.where(row == col, l_ref[...], 0.0), axis=0, keepdims=True)
        inverse_ref[...] = inverse * by_col

    for copy in copies:
        copy.wait()


def product(lh, ll, s_ref, j):
    at = range(4 * j, 4 * j + 4)
    lines = jnp.concatenate([s_ref[pl.ds(k, GROUP, stride=2 * TPC), :] for k in at], axis=1)
    return dot3(lh, ll, *split(lines))


def multiply_first(l_ref, s_ref, out_ref):
    lh, ll = split(l_ref[...].T)
    for j in range(3):
        out_ref[:, j * 512 : (j + 1) * 512] = product(lh, ll, s_ref, j)


def multiply_next(la_ref, sa_ref, lb_ref, sb_ref, acc_ref, out_ref):
    ah, al = split(la_ref[...].T)
    bh, bl = split(lb_ref[...].T)
    for j in range(3):
        at = slice(j * 512, (j + 1) * 512)
        out_ref[:, at] = acc_ref[:, at] + product(ah, al, sa_ref, j) + product(bh, bl, sb_ref, j)


def multiply_last(la_ref, lb_ref, s_ref, acc_ref, _, keep_ref, send_ref):
    x, c, z, y = place()
    lh, ll = split(jnp.concatenate([la_ref[...], lb_ref[...]], axis=0).T)
    turn = 2 * (z % 2) + y // 2
    for j in range(3):
        at = slice(j * 512, (j + 1) * 512)
        part = acc_ref[:, at] + product(lh, ll, s_ref, j)
        turned = part.T.reshape(2, 2, 8, 16, NB)
        for odd in range(2):

            @pl.when((c ^ (y % 2)) == odd)
            def _():
                for i in range(4):
                    away = i ^ turn ^ x
                    near = jnp.where(away == 0, 0, jnp.where(away == 1, 2, jnp.where(away == 3, 1, 3)))
                    far = jnp.where(away == 0, 0, jnp.where(away == 1, 1, jnp.where(away == 3, 2, 3)))
                    mine = jnp.where(c == 0, near, far)
                    other = jnp.where(c == 0, far, near)
                    for v in range(2):
                        keep_ref[mine, 2 * j + v] = turned[v, :, 2 * i + odd]
                        send_ref[other, 2 * j + v] = turned[v, :, 2 * i + 1 - odd]


def add_cores(rows, rows_in, keep_ref, send_ref):
    keep_ref[...] = rows[:2] + rows_in[:2]
    send_ref[...] = rows[2:] + rows_in[2:]


def add_pairs(rows, rows_in, keep_ref, send_ref):
    keep_ref[...] = rows[0] + rows_in[0]
    send_ref[...] = rows[1] + rows_in[1]


def add_rows(rows, rows_in, keep_ref, send_ref):
    high = place()[2] // 2
    keep_ref[...] = rows[:, high] + rows_in[:, high]
    send_ref[...] = rows[:, 1 - high] + rows_in[:, 1 - high]


def join_rows(keep_ref, other_ref, out_ref):
    high = place()[2] // 2
    for v in range(TPC):
        out_ref[2 * v + high] = keep_ref[v]
        out_ref[2 * v + 1 - high] = other_ref[v]


def finish_rows(own_ref, product_ref, inv_ref, out_ref):
    adjusted = own_ref[...] - 2.0 * product_ref[...]
    out_ref[...] = dot6(adjusted.reshape(PIECE, NB), inv_ref[...]).reshape(UR, 16, NB)


def start_panel(share, own_ref, mine_ref, inv_ref, lbar_ref, out_ref):
    row, col = grids()
    gram = tdot6(inv_ref[...], tdot6(own_ref[...].reshape(PIECE, NB), mine_ref[...].reshape(PIECE, NB)))
    out_ref[...] = lbar_ref[...] * share - jnp.where(row >= col, gram, 0.0)


def finish_panel(first_ref, second_ref, l_first_ref, l_second_ref, l_ref, inv_ref, base_ref, keep_ref, send_ref):
    c = place()[1]
    row, col = grids()
    half = PIECE // 2
    cross = tdot6(first_ref[...].reshape(half, NB), l_first_ref[...].reshape(half, NB))
    cross += tdot6(second_ref[...].reshape(half, NB), l_second_ref[...].reshape(half, NB))
    inverse = inv_ref[...]
    fresh = base_ref[...] + jnp.where(row >= col, 2.0 * tdot6(inverse, cross), 0.0)
    phi = tdot6(l_ref[...], fresh)
    phi = jnp.where(row > col, phi, jnp.where(row == col, 0.5 * phi, 0.0))
    full = dot6(tdot6(inverse, phi), inverse)
    result = 0.5 * (full + full.T)
    n = NB // 2
    row, col = row[:n, :n], col[:n, :n]
    last = result[n:, n:]
    mixed = jnp.where(row >= col, result[:n, :n], last)
    diagonal = jnp.sum(jnp.where(row == col, last, 0.0), axis=0, keepdims=True)
    lower = result[n:, :n]
    keep_ref[:n] = jnp.where(c == 0, lower, mixed)
    send_ref[:n] = jnp.where(c == 0, mixed, lower)
    keep_ref[n:] = jnp.broadcast_to(diagonal, (8, n))
    send_ref[n:] = jnp.broadcast_to(diagonal, (8, n))


def add_two(part, other, out_ref):
    out_ref[...] = part[...] + other[...]


def add_four(part, near, opposite, beyond, _, out_ref):
    out_ref[...] = (part[...] + near[...]) + (beyond[...] + opposite[...])


def unpack(part, rest, out_ref):
    c = place()[1]
    n = NB // 2
    row = lax.broadcasted_iota(jnp.int32, (n, n), 0)
    col = lax.broadcasted_iota(jnp.int32, (n, n), 1)
    lower = jnp.where(c == 0, part[:n], rest[:n])
    mixed = jnp.where(c == 0, rest[:n], part[:n])
    diagonal = jnp.where(c == 0, rest[n : n + 1], part[n : n + 1])
    turned = mixed.T
    out_ref[:n, :n] = jnp.where(row >= col, mixed, turned)
    out_ref[n:, n:] = jnp.where(row == col, diagonal, jnp.where(row < col, mixed, turned))
    out_ref[n:, :n] = lower
    out_ref[:n, n:] = lower.T


def shards(l_panel, l_rows, lbar_panel, lbar_rows, sbar):
    share = 1.0 / (lax.axis_size("prow") * lax.axis_size("pcol"))
    s_lines = sbar.reshape(16 * SLAB, 128)
    mine = jnp.transpose(l_rows[0], (1, 0, 2))
    own = jnp.transpose(lbar_rows[0], (1, 0, 2))
    dma = pltpu.SemaphoreType.DMA
    lines = kept(4 * SLAB, 128)
    square = kept(NB, NB)

    (piece,) = call(order_rows, [mine], [free(PIECE, NB)], 4, size=400_000)
    up = permute(piece, first_axis(1))
    down = permute(piece, first_axis(-1))
    s0, s3, strict, blocks, l_kept, lbar_kept, own_kept, mine_kept = call(
        invert_blocks,
        [s_lines, l_panel, lbar_panel, own, mine, up, down],
        [lines, lines, square, square, square, square, kept(UR, 16, NB), kept(UR, 16, NB)],
        4,
        flops=6 * 12 * NB**3,
        size=10_000_000,
        scratch=[dma((2, 4)), dma((4,))],
        specs=[HBM] * 5 + [ANY] * 2,
    )
    far_up = permute(up[: PIECE // 2], first_axis(1))
    far_down = permute(down[PIECE // 2 :], first_axis(-1))
    tile = kept(TPC, 16, NB)
    rows = permute(mine, to_tiles)
    (group,) = call(
        join_group,
        [piece, up, down, far_up, far_down, blocks],
        [free(GROUP, NB)],
        4,
        size=1_600_000,
        specs=[VMEM] * 5 + [ANY],
    )
    group_up = permute(group, second_axis(1))
    group_down = permute(group, second_axis(-1))
    s1, s2, inverse = call(
        invert_rest,
        [s_lines, strict, blocks, l_kept, group],
        [lines, lines, square],
        4,
        flops=8 * 12 * NB**3,
        size=10_000_000,
        scratch=[dma((2, 4))],
        specs=[HBM] + [VMEM] * 3 + [ANY],
    )
    work = dict(flops=6 * GROUP * COLS * NB, size=6_000_000)
    wide = kept(NB, COLS)
    (total,) = call(multiply_first, [group, s0], [wide], 8, **work)
    l_keep, l_send = call(
        split_tiles, [rows, inverse, total], [tile, tile], 4, size=800_000, specs=[VMEM, ANY, ANY]
    )
    l_other = permute(l_send, opposite_half)
    pass_up, pass_down = call(
        take_halves,
        [group_up, group_down, total, l_keep],
        [free(GROUP // 2, NB)] * 2,
        4,
        size=1_000_000,
        specs=[VMEM, VMEM, ANY, ANY],
    )
    far_a = permute(pass_up, second_axis(1))
    far_b = permute(pass_down, second_axis(-1))
    (total,) = call(multiply_next, [group_up, s3, group_down, s1, total], [wide], 8, **work)
    share4 = kept(4, TPC, 2, 16, NB)
    keep, send = call(
        multiply_last, [far_a, far_b, s2, total, l_other], [share4, share4], 8, specs=[VMEM] * 4 + [ANY], **work
    )

    share2 = kept(2, TPC, 2, 16, NB)
    share1 = kept(TPC, 2, 16, NB)
    (base,) = call(
        functools.partial(start_panel, share), [own_kept, mine_kept, inverse, lbar_kept], [square], 6,
        flops=2 * 12 * NB**3, size=4_000_000,
    )
    keep, send = call(add_cores, [keep, permute(send, other_core)], [share2, share2], 6, size=2_000_000)
    keep, send = call(add_pairs, [keep, permute(send, halving(0))], [share1, share1], 6, size=1_000_000)
    keep, send = call(add_rows, [keep, permute(send, halving(1))], [tile, tile], 6, size=1_000_000)
    half = kept(NB // 2 + 8, NB // 2)
    part, other = call(
        finish_panel,
        [keep, send, l_keep, l_other, l_kept, inverse, base],
        [half, half],
        8,
        flops=6 * 12 * NB**3,
        size=4_000_000,
    )

    (rows,) = call(join_rows, [keep, permute(send, opposite_half)], [free(UR, 16, NB)], 4, size=800_000)
    (part,) = call(add_two, [part, permute(other, other_core)], [half], 4, size=500_000)

    def add_around(stage, after):
        others = [permute(part, crossing(stage, mask)) for mask in (1, 3, 2)]
        return call(add_four, [part, *others, after], [half], 4, size=1_000_000, specs=[VMEM] * 4 + [ANY])

    (part,) = add_around(0, rows)
    rows = permute(rows, to_rows)
    (part,) = add_around(1, inverse)
    (part,) = add_around(2, rows)
    (abar,) = call(
        finish_rows,
        [own_kept, rows, inverse],
        [free(UR, 16, NB)],
        6,
        flops=12 * PIECE * NB * NB,
        size=1_000_000,
    )
    rest = permute(part, other_core)
    (abar_panel,) = call(unpack, [part, rest], [free(NB, NB)], 4, size=500_000)
    return jnp.transpose(abar, (1, 0, 2))[None], abar_panel


def solution(mesh):
    return jax.shard_map(
        shards,
        mesh=mesh,
        in_specs=(
            P(),
            P("prow", "pcol", None, None),
            P(),
            P("prow", "pcol", None, None),
            P("prow", None, None, "pcol", None, None),
        ),
        out_specs=(P("prow", "pcol", None, None), P()),
        check_vma=False,
    )
```

```python
import functools

import jax
import jax.numpy as jnp
from jax import lax
from jax.experimental import pallas as pl
from jax.experimental.pallas import tpu as pltpu
from jax.sharding import PartitionSpec as P

F32 = jnp.float32
BF16 = jnp.bfloat16
AXES = ("prow", "pcol")
NB = 256
UR = 12
TPC = 6
PIECE = 16 * UR
GROUP = 4 * PIECE
SLAB = PIECE * TPC * 2
COLS = TPC * NB
VMEM = pl.BlockSpec(memory_space=pltpu.VMEM)
ANY = pl.BlockSpec(memory_space=pl.ANY)
HBM = pl.BlockSpec(memory_space=pltpu.HBM)


def pairs(target):
    found = []
    for x in range(4):
        for c in range(2):
            for z in range(4):
                for y in range(4):
                    tx, tc, tz, ty = target(x, c, z, y)
                    found.append(
                        ((2 * x + c) * 16 + 4 * z + y, (2 * (tx % 4) + tc) * 16 + 4 * (tz % 4) + ty % 4)
                    )
    return found


def permute(value, target):
    return lax.ppermute(value, AXES, pairs(target))


def first_axis(step):
    return lambda x, c, z, y: (x, c, z, y + step) if c == 0 else (x, c, z + step, y)


def second_axis(step):
    return lambda x, c, z, y: (x, c, z + step, y) if c == 0 else (x, c, z, y + step)


def other_core(x, c, z, y):
    return x, 1 - c, z, y


def halving(stage):
    def target(x, c, z, y):
        return (x ^ 1 if (stage + c) % 2 == 0 else x ^ 3), c, z, y

    return target


def crossing(stage, mask):
    def target(x, c, z, y):
        axis = (stage + c) % 3
        if axis == 0:
            return x ^ mask, c, z, y
        if axis == 1:
            return x, c, z, y ^ mask
        return x, c, z ^ mask, y

    return target


def opposite_half(x, c, z, y):
    return x, c, z ^ 2, y


def to_tiles(x, c, z, y):
    p, q = 2 * x + c, 4 * z + y
    tp, tq = (q % 8) ^ p, 8 * (q // 8) + p
    return tp // 2, tp % 2, tq // 4, tq % 4


def to_rows(x, c, z, y):
    p, q = 2 * x + c, 4 * z + y
    tp, tq = q % 8, 8 * (q // 8) + (p ^ (q % 8))
    return tp // 2, tp % 2, tq // 4, tq % 4


def place():
    p, q = lax.axis_index("prow"), lax.axis_index("pcol")
    return p // 2, p % 2, q // 4, q % 4


def split(value):
    high = value.astype(BF16)
    return high, (value - high.astype(F32)).astype(BF16)


def dot3(lh, ll, rh, rl):
    total = jnp.dot(lh, rh, preferred_element_type=F32)
    total += jnp.dot(ll, rh, preferred_element_type=F32)
    total += jnp.dot(lh, rl, preferred_element_type=F32)
    return total


def dot6(left, right):
    return jnp.dot(left, right, precision=lax.Precision.HIGHEST, preferred_element_type=F32)


def tdot6(left, right):
    return lax.dot_general(
        left, right, (((0,), (0,)), ((), ())), precision=lax.Precision.HIGHEST, preferred_element_type=F32
    )


def call(kernel, inputs, outputs, limit, flops=0, size=0, scratch=(), specs=None):
    if specs:
        inputs = [
            pltpu.with_memory_space_constraint(value, pltpu.HBM) if spec is HBM else value
            for value, spec in zip(inputs, specs)
        ]
    return pl.pallas_call(
        kernel,
        in_specs=specs or [VMEM] * len(inputs),
        out_specs=[VMEM] * len(outputs),
        out_shape=list(outputs),
        scratch_shapes=list(scratch),
        compiler_params=pltpu.CompilerParams(vmem_limit_bytes=limit << 20),
        cost_estimate=pl.CostEstimate(flops=flops, bytes_accessed=size, transcendentals=0),
        name=(kernel.func if isinstance(kernel, functools.partial) else kernel).__name__,
    )(*inputs)


def kept(*shape):
    return pltpu.VMEM(shape, F32)


def free(*shape):
    return jax.ShapeDtypeStruct(shape, F32)


def split_tiles(rows_ref, _, keep_ref, send_ref):
    high = place()[2] // 2
    for v in range(TPC):
        keep_ref[v] = rows_ref[2 * v + high]
        send_ref[v] = rows_ref[2 * v + 1 - high]


def join_group(own_ref, up_ref, down_ref, far_ref, _, first_ref, second_ref):
    def ordered(ref):
        return jnp.swapaxes(ref[...], 0, 1).reshape(PIECE, NB)

    first_ref[:PIECE] = ordered(own_ref)
    first_ref[PIECE:] = ordered(up_ref)
    second_ref[:PIECE] = ordered(down_ref)
    second_ref[PIECE:] = ordered(far_ref)


def fetch(step, s_ref, held_ref, sem):
    _, c, z, y = place()
    copies = []
    for i, offset in enumerate((0, 3, 1, 2)):
        zz = jnp.where(c == 0, z + step, z + offset) % 4
        yy = jnp.where(c == 0, y + offset, y + step) % 4
        copy = pltpu.make_async_copy(
            s_ref.at[pl.ds((zz * 4 + yy) * SLAB, SLAB), :],
            held_ref.at[pl.ds(i * SLAB, SLAB), :],
            sem.at[i],
        )
        copy.start()
        copies.append(copy)
    return copies


def grids():
    row = lax.broadcasted_iota(jnp.int32, (NB, NB), 0)
    col = lax.broadcasted_iota(jnp.int32, (NB, NB), 1)
    return row, col


def invert_blocks(
    s_ref, l_ref, lbar_ref, own_ref, mine_ref,
    first_s, second_s, strict_ref, inverse_ref, l_out, lbar_out, own_out, mine_out, sem, small,
):
    panel = pltpu.make_async_copy(l_ref, l_out, small.at[0])
    panel.start()
    copies = fetch(0, s_ref, first_s, sem.at[0])
    for i, (src, dst) in enumerate(((lbar_ref, lbar_out), (own_ref, own_out), (mine_ref, mine_out))):
        copy = pltpu.make_async_copy(src, dst, small.at[i + 1])
        copy.start()
        copies.append(copy)
    copies += fetch(3, s_ref, second_s, sem.at[1])
    panel.wait()
    row, col = grids()
    lower = l_out[...]
    by_row = 1.0 / jnp.sum(jnp.where(row == col, lower, 0.0), axis=1, keepdims=True)
    strict = jnp.where(row > col, lower * by_row, 0.0)
    power = jnp.where(row // 16 == col // 16, -strict, 0.0)
    inverse = jnp.where(row == col, 1.0, 0.0) + power
    for _ in range(3):
        power = dot6(power, power)
        inverse = inverse + dot6(power, inverse)
    strict_ref[...] = strict
    inverse_ref[...] = inverse
    for copy in copies:
        copy.wait()


def invert_rest(strict_ref, blocks_ref, l_ref, _, inverse_ref):
    row, col = grids()
    strict = strict_ref[...]
    inverse = blocks_ref[...]
    size = 16
    while size < NB:
        beside = (row // (2 * size) == col // (2 * size)) & (row // size != col // size)
        inverse = inverse - dot6(inverse, dot6(jnp.where(beside, strict, 0.0), inverse))
        size *= 2
    inverse_ref[...] = inverse * (1.0 / jnp.sum(jnp.where(row == col, l_ref[...], 0.0), axis=0, keepdims=True))


def product(lh, ll, s_ref, j):
    at = range(4 * j, 4 * j + 4)
    lines = jnp.concatenate([s_ref[pl.ds(k, GROUP, stride=2 * TPC), :] for k in at], axis=1)
    return dot3(lh, ll, *split(lines))


def beside_copies(copies, compute):
    pl.when(place()[0] >= 0)(compute)
    for copy in copies:
        copy.wait()


def parts(first_ref, second_ref):
    return split(jnp.concatenate([first_ref[...], second_ref[...]], axis=0).T)


def multiply_first(la_ref, lb_ref, s_ref, s_all_ref, out_ref, next_ref, sem):
    def compute():
        lh, ll = parts(la_ref, lb_ref)
        for j in range(3):
            out_ref[:, j * 512 : (j + 1) * 512] = product(lh, ll, s_ref, j)

    beside_copies(fetch(1, s_all_ref, next_ref, sem), compute)


def multiply_up(la_ref, lb_ref, s_ref, acc_ref, s_all_ref, out_ref, next_ref, sem):
    def compute():
        lh, ll = parts(la_ref, lb_ref)
        for j in range(3):
            at = slice(j * 512, (j + 1) * 512)
            out_ref[:, at] = acc_ref[:, at] + product(lh, ll, s_ref, j)

    beside_copies(fetch(2, s_all_ref, next_ref, sem), compute)


def multiply_down(la_ref, lb_ref, s_ref, acc_ref, _, out_ref):
    lh, ll = parts(la_ref, lb_ref)
    for j in range(3):
        at = slice(j * 512, (j + 1) * 512)
        out_ref[:, at] = acc_ref[:, at] + product(lh, ll, s_ref, j)


def multiply_last(la_ref, lb_ref, s_ref, acc_ref, keep_ref, send_ref):
    x, c, z, y = place()
    lh, ll = parts(la_ref, lb_ref)
    turn = 2 * (z % 2) + y // 2
    for j in range(3):
        at = slice(j * 512, (j + 1) * 512)
        part = acc_ref[:, at] + product(lh, ll, s_ref, j)
        turned = part.T.reshape(2, 2, 8, 16, NB)
        for odd in range(2):

            @pl.when((c ^ (y % 2)) == odd)
            def _():
                for i in range(4):
                    away = i ^ turn ^ x
                    near = jnp.where(away == 0, 0, jnp.where(away == 1, 2, jnp.where(away == 3, 1, 3)))
                    far = jnp.where(away == 0, 0, jnp.where(away == 1, 1, jnp.where(away == 3, 2, 3)))
                    mine = jnp.where(c == 0, near, far)
                    other = jnp.where(c == 0, far, near)
                    for v in range(2):
                        keep_ref[mine, 2 * j + v] = turned[v, :, 2 * i + odd]
                        send_ref[other, 2 * j + v] = turned[v, :, 2 * i + 1 - odd]


def add_cores(rows, rows_in, keep_ref, send_ref):
    keep_ref[...] = rows[:2] + rows_in[:2]
    send_ref[...] = rows[2:] + rows_in[2:]


def add_pairs(rows, rows_in, _, __, keep_ref, send_ref):
    keep_ref[...] = rows[0] + rows_in[0]
    send_ref[...] = rows[1] + rows_in[1]


def add_rows(rows, rows_in, keep_ref, send_ref):
    high = place()[2] // 2
    keep_ref[...] = rows[:, high] + rows_in[:, high]
    send_ref[...] = rows[:, 1 - high] + rows_in[:, 1 - high]


def join_rows(keep_ref, other_ref, out_ref):
    high = place()[2] // 2
    for v in range(TPC):
        out_ref[2 * v + high] = keep_ref[v]
        out_ref[2 * v + 1 - high] = other_ref[v]


def finish_rows(own_ref, product_ref, inv_ref, out_ref):
    adjusted = own_ref[...] - 2.0 * product_ref[...]
    out_ref[...] = dot6(adjusted.reshape(PIECE, NB), inv_ref[...]).reshape(UR, 16, NB)


def start_panel(share, own_ref, mine_ref, inv_ref, lbar_ref, out_ref):
    row, col = grids()
    gram = tdot6(inv_ref[...], tdot6(own_ref[...].reshape(PIECE, NB), mine_ref[...].reshape(PIECE, NB)))
    out_ref[...] = lbar_ref[...] * share - jnp.where(row >= col, gram, 0.0)


def finish_panel(
    first_ref, second_ref, l_first_ref, l_second_ref, l_ref, inv_ref, base_ref, keep_ref, send_ref, second_out
):
    c = place()[1]
    row, col = grids()
    half = PIECE // 2
    cross = tdot6(first_ref[...].reshape(half, NB), l_first_ref[...].reshape(half, NB))
    cross += tdot6(second_ref[...].reshape(half, NB), l_second_ref[...].reshape(half, NB))
    inverse = inv_ref[...]
    fresh = base_ref[...] + jnp.where(row >= col, 2.0 * tdot6(inverse, cross), 0.0)
    phi = tdot6(l_ref[...], fresh)
    phi = jnp.where(row > col, phi, jnp.where(row == col, 0.5 * phi, 0.0))
    full = dot6(tdot6(inverse, phi), inverse)
    result = 0.5 * (full + full.T)
    n = NB // 2
    row, col = row[:n, :n], col[:n, :n]
    last = result[n:, n:]
    mixed = jnp.where(row >= col, result[:n, :n], last)
    diagonal = jnp.sum(jnp.where(row == col, last, 0.0), axis=0, keepdims=True)
    lower = result[n:, :n]
    keep_ref[:n] = jnp.where(c == 0, lower, mixed)
    send_ref[:n] = jnp.where(c == 0, mixed, lower)
    keep_ref[n:] = jnp.broadcast_to(diagonal, (8, n))
    send_ref[n:] = jnp.broadcast_to(diagonal, (8, n))
    second_out[...] = second_ref[...]


def add_two(part, other, out_ref):
    out_ref[...] = part[...] + other[...]


def add_four(part, near, opposite, beyond, _, out_ref):
    out_ref[...] = (part[...] + near[...]) + (beyond[...] + opposite[...])


def unpack(part, rest, out_ref):
    c = place()[1]
    n = NB // 2
    row = lax.broadcasted_iota(jnp.int32, (n, n), 0)
    col = lax.broadcasted_iota(jnp.int32, (n, n), 1)
    lower = jnp.where(c == 0, part[:n], rest[:n])
    mixed = jnp.where(c == 0, rest[:n], part[:n])
    diagonal = jnp.where(c == 0, rest[n : n + 1], part[n : n + 1])
    turned = mixed.T
    out_ref[:n, :n] = jnp.where(row >= col, mixed, turned)
    out_ref[n:, n:] = jnp.where(row == col, diagonal, jnp.where(row < col, mixed, turned))
    out_ref[n:, :n] = lower
    out_ref[:n, n:] = lower.T


def shards(l_panel, l_rows, lbar_panel, lbar_rows, sbar):
    share = 1.0 / (lax.axis_size("prow") * lax.axis_size("pcol"))
    s_lines = sbar.reshape(16 * SLAB, 128)
    mine = jnp.transpose(l_rows[0], (1, 0, 2))
    own = jnp.transpose(lbar_rows[0], (1, 0, 2))
    dma = pltpu.SemaphoreType.DMA
    lines = kept(4 * SLAB, 128)
    square = kept(NB, NB)

    up = permute(mine, first_axis(1))
    down = permute(mine, first_axis(-1))
    far = permute(mine, first_axis(2))
    s0, s3, strict, blocks, l_kept, lbar_kept, own_kept, mine_kept = call(
        invert_blocks,
        [s_lines, l_panel, lbar_panel, own, mine],
        [lines, lines, square, square, square, square, kept(UR, 16, NB), kept(UR, 16, NB)],
        4,
        flops=6 * 12 * NB**3,
        size=10_000_000,
        scratch=[dma((2, 4)), dma((4,))],
        specs=[HBM] * 5,
    )
    tile = kept(TPC, 16, NB)
    rows = permute(mine, to_tiles)
    first, second = call(
        join_group,
        [mine_kept, up, down, far, blocks],
        [free(GROUP // 2, NB)] * 2,
        4,
        size=1_600_000,
        specs=[VMEM] * 4 + [ANY],
    )
    up_first = permute(first, second_axis(1))
    down_second = permute(second, second_axis(-1))
    up_second = permute(second, second_axis(1))
    down_first = permute(first, second_axis(-1))
    far_first = permute(up_first, second_axis(1))
    far_second = permute(down_second, second_axis(-1))
    work = dict(flops=6 * GROUP * COLS * NB, size=6_000_000)
    wide = kept(NB, COLS)
    total, s1 = call(
        multiply_first,
        [first, second, s0, s_lines],
        [wide, lines],
        8,
        scratch=[dma((4,))],
        specs=[VMEM] * 3 + [HBM],
        **work,
    )
    l_keep, l_send = call(split_tiles, [rows, total], [tile, tile], 4, size=800_000, specs=[VMEM, ANY])
    l_other = permute(l_send, opposite_half)
    total, s2 = call(
        multiply_up,
        [up_first, up_second, s3, total, s_lines],
        [wide, lines],
        8,
        scratch=[dma((4,))],
        specs=[VMEM] * 4 + [HBM],
        **work,
    )
    (total,) = call(
        multiply_down,
        [down_first, down_second, s1, total, rows],
        [wide],
        8,
        specs=[VMEM] * 4 + [ANY],
        **work,
    )
    share4 = kept(4, TPC, 2, 16, NB)
    keep, send = call(multiply_last, [far_first, far_second, s2, total], [share4, share4], 8, **work)

    share2 = kept(2, TPC, 2, 16, NB)
    share1 = kept(TPC, 2, 16, NB)
    keep, send = call(add_cores, [keep, permute(send, other_core)], [share2, share2], 6, size=2_000_000)
    (inverse,) = call(
        invert_rest,
        [strict, blocks, l_kept, keep],
        [square],
        6,
        flops=8 * 12 * NB**3,
        size=6_000_000,
        specs=[VMEM] * 3 + [ANY],
    )
    keep, send = call(
        add_pairs,
        [keep, permute(send, halving(0)), inverse, l_other],
        [share1, share1],
        6,
        size=1_000_000,
        specs=[VMEM] * 2 + [ANY] * 2,
    )
    (base,) = call(
        functools.partial(start_panel, share), [own_kept, mine_kept, inverse, lbar_kept], [square], 6,
        flops=2 * 12 * NB**3, size=4_000_000,
    )
    keep, send = call(add_rows, [keep, permute(send, halving(1))], [tile, tile], 6, size=1_000_000)
    half = kept(NB // 2 + 8, NB // 2)
    part, other, send = call(
        finish_panel,
        [keep, send, l_keep, l_other, l_kept, inverse, base],
        [half, half, tile],
        8,
        flops=6 * 12 * NB**3,
        size=4_000_000,
    )

    (rows,) = call(join_rows, [keep, permute(send, opposite_half)], [free(UR, 16, NB)], 4, size=800_000)
    (part,) = call(add_two, [part, permute(other, other_core)], [half], 4, size=500_000)

    def add_around(stage, after):
        others = [permute(part, crossing(stage, mask)) for mask in (1, 3, 2)]
        return call(add_four, [part, *others, after], [half], 4, size=1_000_000, specs=[VMEM] * 4 + [ANY])

    (part,) = add_around(0, rows)
    rows = permute(rows, to_rows)
    (part,) = add_around(1, inverse)
    (part,) = add_around(2, rows)
    (abar,) = call(
        finish_rows,
        [own_kept, rows, inverse],
        [free(UR, 16, NB)],
        6,
        flops=12 * PIECE * NB * NB,
        size=1_000_000,
    )
    rest = permute(part, other_core)
    (abar_panel,) = call(unpack, [part, rest], [free(NB, NB)], 4, size=500_000)
    return jnp.transpose(abar, (1, 0, 2))[None], abar_panel


def solution(mesh):
    return jax.shard_map(
        shards,
        mesh=mesh,
        in_specs=(
            P(),
            P("prow", "pcol", None, None),
            P(),
            P("prow", "pcol", None, None),
            P("prow", None, None, "pcol", None, None),
        ),
        out_specs=(P("prow", "pcol", None, None), P()),
        check_vma=False,
    )
```

```python
import functools

import jax
import jax.numpy as jnp
from jax import lax
from jax.experimental import pallas as pl
from jax.experimental.pallas import tpu as pltpu
from jax.sharding import PartitionSpec as P

F32 = jnp.float32
BF16 = jnp.bfloat16
AXES = ("prow", "pcol")
NB = 256
UR = 12
TPC = 6
PIECE = 16 * UR
GROUP = 4 * PIECE
SLAB = PIECE * TPC * 2
COLS = TPC * NB
VMEM = pl.BlockSpec(memory_space=pltpu.VMEM)
ANY = pl.BlockSpec(memory_space=pl.ANY)
HBM = pl.BlockSpec(memory_space=pltpu.HBM)


def pairs(target):
    found = []
    for x in range(4):
        for c in range(2):
            for z in range(4):
                for y in range(4):
                    tx, tc, tz, ty = target(x, c, z, y)
                    found.append(
                        ((2 * x + c) * 16 + 4 * z + y, (2 * (tx % 4) + tc) * 16 + 4 * (tz % 4) + ty % 4)
                    )
    return found


def permute(value, target):
    return lax.ppermute(value, AXES, pairs(target))


def first_axis(step):
    return lambda x, c, z, y: (x, c, z, y + step) if c == 0 else (x, c, z + step, y)


def second_axis(step):
    return lambda x, c, z, y: (x, c, z + step, y) if c == 0 else (x, c, z, y + step)


def other_core(x, c, z, y):
    return x, 1 - c, z, y


def halving(stage):
    def target(x, c, z, y):
        return (x ^ 1 if (stage + c) % 2 == 0 else x ^ 3), c, z, y

    return target


def crossing(stage, mask):
    def target(x, c, z, y):
        if stage == 2:
            return x ^ mask, c, z, y
        if stage == c:
            return x, c, z, y ^ mask
        return x, c, z ^ mask, y

    return target


def opposite_half(x, c, z, y):
    return x, c, z ^ 2, y


def to_tiles(x, c, z, y):
    p, q = 2 * x + c, 4 * z + y
    tp, tq = (q % 8) ^ p, 8 * (q // 8) + p
    return tp // 2, tp % 2, tq // 4, tq % 4


def to_rows(x, c, z, y):
    p, q = 2 * x + c, 4 * z + y
    tp, tq = q % 8, 8 * (q // 8) + (p ^ (q % 8))
    return tp // 2, tp % 2, tq // 4, tq % 4


def place():
    p, q = lax.axis_index("prow"), lax.axis_index("pcol")
    return p // 2, p % 2, q // 4, q % 4


def split(value):
    high = value.astype(BF16)
    return high, (value - high.astype(F32)).astype(BF16)


def dot3(lh, ll, rh, rl):
    total = jnp.dot(lh, rh, preferred_element_type=F32)
    total += jnp.dot(ll, rh, preferred_element_type=F32)
    total += jnp.dot(lh, rl, preferred_element_type=F32)
    return total


def dot6(left, right):
    return jnp.dot(left, right, precision=lax.Precision.HIGHEST, preferred_element_type=F32)


def tdot6(left, right):
    return lax.dot_general(
        left, right, (((0,), (0,)), ((), ())), precision=lax.Precision.HIGHEST, preferred_element_type=F32
    )


def call(kernel, inputs, outputs, limit, flops=0, size=0, scratch=(), specs=None):
    if specs:
        inputs = [
            pltpu.with_memory_space_constraint(value, pltpu.HBM) if spec is HBM else value
            for value, spec in zip(inputs, specs)
        ]
    return pl.pallas_call(
        kernel,
        in_specs=specs or [VMEM] * len(inputs),
        out_specs=[VMEM] * len(outputs),
        out_shape=list(outputs),
        scratch_shapes=list(scratch),
        compiler_params=pltpu.CompilerParams(vmem_limit_bytes=limit << 20),
        cost_estimate=pl.CostEstimate(flops=flops, bytes_accessed=size, transcendentals=0),
        name=(kernel.func if isinstance(kernel, functools.partial) else kernel).__name__,
    )(*inputs)


def kept(*shape):
    return pltpu.VMEM(shape, F32)


def free(*shape):
    return jax.ShapeDtypeStruct(shape, F32)


def split_tiles(rows_ref, _, keep_ref, send_ref):
    high = place()[2] // 2
    for v in range(TPC):
        keep_ref[v] = rows_ref[2 * v + high]
        send_ref[v] = rows_ref[2 * v + 1 - high]


def join_group(own_ref, up_ref, down_ref, far_ref, _, first_ref, second_ref):
    def ordered(ref):
        return jnp.swapaxes(ref[...], 0, 1).reshape(PIECE, NB)

    first_ref[:PIECE] = ordered(own_ref)
    first_ref[PIECE:] = ordered(up_ref)
    second_ref[:PIECE] = ordered(down_ref)
    second_ref[PIECE:] = ordered(far_ref)


def fetch(step, s_ref, held_ref, sem):
    _, c, z, y = place()
    copies = []
    for i, offset in enumerate((0, 3, 1, 2)):
        zz = jnp.where(c == 0, z + step, z + offset) % 4
        yy = jnp.where(c == 0, y + offset, y + step) % 4
        copy = pltpu.make_async_copy(
            s_ref.at[pl.ds((zz * 4 + yy) * SLAB, SLAB), :],
            held_ref.at[pl.ds(i * SLAB, SLAB), :],
            sem.at[i],
        )
        copy.start()
        copies.append(copy)
    return copies


def grids():
    row = lax.broadcasted_iota(jnp.int32, (NB, NB), 0)
    col = lax.broadcasted_iota(jnp.int32, (NB, NB), 1)
    return row, col


def invert_blocks(
    s_ref, l_ref, lbar_ref, own_ref, mine_ref,
    first_s, second_s, strict_ref, inverse_ref, l_out, lbar_out, own_out, mine_out, sem, small,
):
    panel = pltpu.make_async_copy(l_ref, l_out, small.at[0])
    panel.start()
    copies = fetch(0, s_ref, first_s, sem.at[0])
    for i, (src, dst) in enumerate(((lbar_ref, lbar_out), (own_ref, own_out), (mine_ref, mine_out))):
        copy = pltpu.make_async_copy(src, dst, small.at[i + 1])
        copy.start()
        copies.append(copy)
    copies += fetch(3, s_ref, second_s, sem.at[1])
    panel.wait()
    row, col = grids()
    lower = l_out[...]
    by_row = 1.0 / jnp.sum(jnp.where(row == col, lower, 0.0), axis=1, keepdims=True)
    strict = jnp.where(row > col, lower * by_row, 0.0)
    power = jnp.where(row // 16 == col // 16, -strict, 0.0)
    inverse = jnp.where(row == col, 1.0, 0.0) + power
    for _ in range(3):
        power = dot6(power, power)
        inverse = inverse + dot6(power, inverse)
    strict_ref[...] = strict
    inverse_ref[...] = inverse
    for copy in copies:
        copy.wait()


def invert_rest(strict_ref, blocks_ref, l_ref, _, inverse_ref):
    n = NB // 2
    row = lax.broadcasted_iota(jnp.int32, (n, n), 0)
    col = lax.broadcasted_iota(jnp.int32, (n, n), 1)
    strict = [strict_ref[:n, :n], strict_ref[n:, n:]]
    inverse = [blocks_ref[:n, :n], blocks_ref[n:, n:]]
    size = 16
    while size < n:
        beside = (row // (2 * size) == col // (2 * size)) & (row // size != col // size)
        inner = [dot6(jnp.where(beside, strict[i], 0.0), inverse[i]) for i in range(2)]
        inverse = [inverse[i] - dot6(inverse[i], inner[i]) for i in range(2)]
        size *= 2
    below = -dot6(inverse[1], dot6(strict_ref[n:, :n], inverse[0]))
    diagonal = [jnp.where(row == col, l_ref[at : at + n, at : at + n], 0.0) for at in (0, n)]
    by_col = [1.0 / jnp.sum(value, axis=0, keepdims=True) for value in diagonal]
    inverse_ref[:n, :n] = inverse[0] * by_col[0]
    inverse_ref[:n, n:] = jnp.zeros((n, n), F32)
    inverse_ref[n:, :n] = below * by_col[0]
    inverse_ref[n:, n:] = inverse[1] * by_col[1]


def product(lh, ll, s_ref, j):
    at = range(4 * j, 4 * j + 4)
    lines = jnp.concatenate([s_ref[pl.ds(k, GROUP, stride=2 * TPC), :] for k in at], axis=1)
    return dot3(lh, ll, *split(lines))


def beside_copies(copies, compute):
    pl.when(place()[0] >= 0)(compute)
    for copy in copies:
        copy.wait()


def parts(first_ref, second_ref):
    return split(jnp.concatenate([first_ref[...], second_ref[...]], axis=0).T)


def multiply_first(la_ref, lb_ref, s_ref, s_all_ref, out_ref, next_ref, sem):
    def compute():
        lh, ll = parts(la_ref, lb_ref)
        for j in range(3):
            out_ref[:, j * 512 : (j + 1) * 512] = product(lh, ll, s_ref, j)

    beside_copies(fetch(1, s_all_ref, next_ref, sem), compute)


def multiply_up(la_ref, lb_ref, s_ref, acc_ref, s_all_ref, out_ref, next_ref, sem):
    def compute():
        lh, ll = parts(la_ref, lb_ref)
        for j in range(3):
            at = slice(j * 512, (j + 1) * 512)
            out_ref[:, at] = acc_ref[:, at] + product(lh, ll, s_ref, j)

    beside_copies(fetch(2, s_all_ref, next_ref, sem), compute)


def multiply_down(la_ref, lb_ref, s_ref, acc_ref, _, out_ref):
    lh, ll = parts(la_ref, lb_ref)
    for j in range(3):
        at = slice(j * 512, (j + 1) * 512)
        out_ref[:, at] = acc_ref[:, at] + product(lh, ll, s_ref, j)


def multiply_last(la_ref, lb_ref, s_ref, acc_ref, keep_ref, send_ref):
    x, c, z, y = place()
    lh, ll = parts(la_ref, lb_ref)
    turn = 2 * (z % 2) + y // 2
    for j in range(3):
        at = slice(j * 512, (j + 1) * 512)
        part = acc_ref[:, at] + product(lh, ll, s_ref, j)
        turned = part.T.reshape(2, 2, 8, 16, NB)
        for odd in range(2):

            @pl.when((c ^ (y % 2)) == odd)
            def _():
                for i in range(4):
                    away = i ^ turn ^ x
                    near = jnp.where(away == 0, 0, jnp.where(away == 1, 2, jnp.where(away == 3, 1, 3)))
                    far = jnp.where(away == 0, 0, jnp.where(away == 1, 1, jnp.where(away == 3, 2, 3)))
                    mine = jnp.where(c == 0, near, far)
                    other = jnp.where(c == 0, far, near)
                    for v in range(2):
                        keep_ref[mine, 2 * j + v] = turned[v, :, 2 * i + odd]
                        send_ref[other, 2 * j + v] = turned[v, :, 2 * i + 1 - odd]


def add_cores(rows, rows_in, keep_ref, send_ref):
    keep_ref[...] = rows[:2] + rows_in[:2]
    send_ref[...] = rows[2:] + rows_in[2:]


def add_pairs(rows, rows_in, _, __, keep_ref, send_ref):
    keep_ref[...] = rows[0] + rows_in[0]
    send_ref[...] = rows[1] + rows_in[1]


def add_rows(rows, rows_in, keep_ref, send_ref):
    high = place()[2] // 2
    keep_ref[...] = rows[:, high] + rows_in[:, high]
    send_ref[...] = rows[:, 1 - high] + rows_in[:, 1 - high]


def join_rows(keep_ref, other_ref, out_ref):
    high = place()[2] // 2
    for v in range(TPC):
        out_ref[2 * v + high] = keep_ref[v]
        out_ref[2 * v + 1 - high] = other_ref[v]


def finish_rows(own_ref, product_ref, inv_ref, out_ref):
    adjusted = own_ref[...] - 2.0 * product_ref[...]
    out_ref[...] = dot6(adjusted.reshape(PIECE, NB), inv_ref[...]).reshape(UR, 16, NB)


def start_panel(share, own_ref, mine_ref, inv_ref, lbar_ref, l_ref, out_ref, inv_t_ref, l_t_ref):
    row, col = grids()
    inv_t = inv_ref[...].T
    inv_t_ref[...] = inv_t
    l_t_ref[...] = l_ref[...].T
    gram = dot6(inv_t, tdot6(own_ref[...].reshape(PIECE, NB), mine_ref[...].reshape(PIECE, NB)))
    out_ref[...] = lbar_ref[...] * share - jnp.where(row >= col, gram, 0.0)


def finish_panel(
    first_ref, second_ref, l_first_ref, l_second_ref, l_t_ref, inv_t_ref, inv_ref, base_ref, keep_ref, send_ref, second_out
):
    c = place()[1]
    row, col = grids()
    half = PIECE // 2
    cross = tdot6(first_ref[...].reshape(half, NB), l_first_ref[...].reshape(half, NB))
    cross += tdot6(second_ref[...].reshape(half, NB), l_second_ref[...].reshape(half, NB))
    inverse = inv_ref[...]
    inv_t = inv_t_ref[...]
    fresh = base_ref[...] + jnp.where(row >= col, 2.0 * dot6(inv_t, cross), 0.0)
    phi = dot6(l_t_ref[...], fresh)
    phi = jnp.where(row > col, phi, jnp.where(row == col, 0.5 * phi, 0.0))
    full = dot6(dot6(inv_t, phi), inverse)
    result = 0.5 * (full + full.T)
    n = NB // 2
    row, col = row[:n, :n], col[:n, :n]
    last = result[n:, n:]
    mixed = jnp.where(row >= col, result[:n, :n], last)
    diagonal = jnp.sum(jnp.where(row == col, last, 0.0), axis=0, keepdims=True)
    lower = result[n:, :n]
    keep_ref[:n] = jnp.where(c == 0, lower, mixed)
    send_ref[:n] = jnp.where(c == 0, mixed, lower)
    keep_ref[n:] = jnp.broadcast_to(diagonal, (8, n))
    send_ref[n:] = jnp.broadcast_to(diagonal, (8, n))
    second_out[...] = second_ref[...]


def add_two(part, other, out_ref):
    out_ref[...] = part[...] + other[...]


def add_four(part, beyond, near, opposite, _, out_ref):
    out_ref[...] = (part[...] + near[...]) + (beyond[...] + opposite[...])


def unpack(part, rest, out_ref):
    c = place()[1]
    n = NB // 2
    row = lax.broadcasted_iota(jnp.int32, (n, n), 0)
    col = lax.broadcasted_iota(jnp.int32, (n, n), 1)
    lower = jnp.where(c == 0, part[:n], rest[:n])
    mixed = jnp.where(c == 0, rest[:n], part[:n])
    diagonal = jnp.where(c == 0, rest[n : n + 1], part[n : n + 1])
    turned = mixed.T
    out_ref[:n, :n] = jnp.where(row >= col, mixed, turned)
    out_ref[n:, n:] = jnp.where(row == col, diagonal, jnp.where(row < col, mixed, turned))
    out_ref[n:, :n] = lower
    out_ref[:n, n:] = lower.T


def shards(l_panel, l_rows, lbar_panel, lbar_rows, sbar):
    share = 1.0 / (lax.axis_size("prow") * lax.axis_size("pcol"))
    s_lines = sbar.reshape(16 * SLAB, 128)
    mine = jnp.transpose(l_rows[0], (1, 0, 2))
    own = jnp.transpose(lbar_rows[0], (1, 0, 2))
    dma = pltpu.SemaphoreType.DMA
    lines = kept(4 * SLAB, 128)
    square = kept(NB, NB)

    far = permute(mine, first_axis(2))
    up = permute(mine, first_axis(1))
    down = permute(mine, first_axis(-1))
    s0, s3, strict, blocks, l_kept, lbar_kept, own_kept, mine_kept = call(
        invert_blocks,
        [s_lines, l_panel, lbar_panel, own, mine],
        [lines, lines, square, square, square, square, kept(UR, 16, NB), kept(UR, 16, NB)],
        4,
        flops=6 * 12 * NB**3,
        size=10_000_000,
        scratch=[dma((2, 4)), dma((4,))],
        specs=[HBM] * 5,
    )
    tile = kept(TPC, 16, NB)
    rows = permute(mine, to_tiles)
    first, second = call(
        join_group,
        [mine_kept, up, down, far, blocks],
        [free(GROUP // 2, NB)] * 2,
        4,
        size=1_600_000,
        specs=[VMEM] * 4 + [ANY],
    )
    up_first = permute(first, second_axis(1))
    down_second = permute(second, second_axis(-1))
    up_second = permute(second, second_axis(1))
    down_first = permute(first, second_axis(-1))
    far_first = permute(up_first, second_axis(1))
    far_second = permute(down_second, second_axis(-1))
    work = dict(flops=6 * GROUP * COLS * NB, size=6_000_000)
    wide = kept(NB, COLS)
    total, s1 = call(
        multiply_first,
        [first, second, s0, s_lines],
        [wide, lines],
        8,
        scratch=[dma((4,))],
        specs=[VMEM] * 3 + [HBM],
        **work,
    )
    l_keep, l_send = call(split_tiles, [rows, total], [tile, tile], 4, size=800_000, specs=[VMEM, ANY])
    l_other = permute(l_send, opposite_half)
    total, s2 = call(
        multiply_up,
        [up_first, up_second, s3, total, s_lines],
        [wide, lines],
        8,
        scratch=[dma((4,))],
        specs=[VMEM] * 4 + [HBM],
        **work,
    )
    (total,) = call(
        multiply_down,
        [down_first, down_second, s1, total, rows],
        [wide],
        8,
        specs=[VMEM] * 4 + [ANY],
        **work,
    )
    share4 = kept(4, TPC, 2, 16, NB)
    keep, send = call(multiply_last, [far_first, far_second, s2, total], [share4, share4], 8, **work)

    share2 = kept(2, TPC, 2, 16, NB)
    share1 = kept(TPC, 2, 16, NB)
    keep, send = call(add_cores, [keep, permute(send, other_core)], [share2, share2], 6, size=2_000_000)
    (inverse,) = call(
        invert_rest,
        [strict, blocks, l_kept, keep],
        [square],
        6,
        flops=8 * 12 * NB**3,
        size=6_000_000,
        specs=[VMEM] * 3 + [ANY],
    )
    keep, send = call(
        add_pairs,
        [keep, permute(send, halving(0)), inverse, l_other],
        [share1, share1],
        6,
        size=1_000_000,
        specs=[VMEM] * 2 + [ANY] * 2,
    )
    base, inv_t, l_t = call(
        functools.partial(start_panel, share), [own_kept, mine_kept, inverse, lbar_kept, l_kept], [square] * 3, 6,
        flops=2 * 12 * NB**3, size=4_000_000,
    )
    keep, send = call(add_rows, [keep, permute(send, halving(1))], [tile, tile], 6, size=1_000_000)
    half = kept(NB // 2 + 8, NB // 2)
    part, other, send = call(
        finish_panel,
        [keep, send, l_keep, l_other, l_t, inv_t, inverse, base],
        [half, half, tile],
        8,
        flops=6 * 12 * NB**3,
        size=4_000_000,
    )

    (rows,) = call(join_rows, [keep, permute(send, opposite_half)], [free(UR, 16, NB)], 4, size=800_000)
    (part,) = call(add_two, [part, permute(other, other_core)], [half], 4, size=500_000)

    def add_around(stage, after):
        others = [permute(part, crossing(stage, mask)) for mask in (2, 1, 3)]
        return call(add_four, [part, *others, after], [half], 4, size=1_000_000, specs=[VMEM] * 4 + [ANY])

    (part,) = add_around(0, rows)
    rows = permute(rows, to_rows)
    (part,) = add_around(1, inverse)
    (part,) = add_around(2, inverse)
    (abar,) = call(
        finish_rows,
        [own_kept, rows, inverse],
        [free(UR, 16, NB)],
        6,
        flops=12 * PIECE * NB * NB,
        size=1_000_000,
    )
    rest = permute(part, other_core)
    (abar_panel,) = call(unpack, [part, rest], [free(NB, NB)], 4, size=500_000)
    return jnp.transpose(abar, (1, 0, 2))[None], abar_panel


def solution(mesh):
    return jax.shard_map(
        shards,
        mesh=mesh,
        in_specs=(
            P(),
            P("prow", "pcol", None, None),
            P(),
            P("prow", "pcol", None, None),
            P("prow", None, None, "pcol", None, None),
        ),
        out_specs=(P("prow", "pcol", None, None), P()),
        check_vma=False,
    )
```

```python
import functools

import jax
import jax.numpy as jnp
from jax import lax
from jax.experimental import pallas as pl
from jax.experimental.pallas import tpu as pltpu
from jax.sharding import PartitionSpec as P

F32 = jnp.float32
BF16 = jnp.bfloat16
AXES = ("prow", "pcol")
NB = 256
UR = 12
TPC = 6
PIECE = 16 * UR
GROUP = 4 * PIECE
SLAB = PIECE * TPC * 2
COLS = TPC * NB
VMEM = pl.BlockSpec(memory_space=pltpu.VMEM)
ANY = pl.BlockSpec(memory_space=pl.ANY)
HBM = pl.BlockSpec(memory_space=pltpu.HBM)


def pairs(target):
    found = []
    for x in range(4):
        for c in range(2):
            for z in range(4):
                for y in range(4):
                    tx, tc, tz, ty = target(x, c, z, y)
                    found.append(
                        ((2 * x + c) * 16 + 4 * z + y, (2 * (tx % 4) + tc) * 16 + 4 * (tz % 4) + ty % 4)
                    )
    return found


def permute(value, target):
    return lax.ppermute(value, AXES, pairs(target))


def first_axis(step):
    return lambda x, c, z, y: (x, c, z, y + step) if c == 0 else (x, c, z + step, y)


def second_axis(step):
    return lambda x, c, z, y: (x, c, z + step, y) if c == 0 else (x, c, z, y + step)


def other_core(x, c, z, y):
    return x, 1 - c, z, y


def halving(stage):
    def target(x, c, z, y):
        return (x ^ 1 if (stage + c) % 2 == 0 else x ^ 3), c, z, y

    return target


def crossing(stage, mask):
    def target(x, c, z, y):
        if stage == 2:
            return x ^ mask, c, z, y
        if stage == c:
            return x, c, z, y ^ mask
        return x, c, z ^ mask, y

    return target


def opposite_half(x, c, z, y):
    return x, c, z ^ 2, y


def to_tiles(x, c, z, y):
    p, q = 2 * x + c, 4 * z + y
    tp, tq = (q % 8) ^ p, 8 * (q // 8) + p
    return tp // 2, tp % 2, tq // 4, tq % 4


def to_rows(x, c, z, y):
    p, q = 2 * x + c, 4 * z + y
    tp, tq = q % 8, 8 * (q // 8) + (p ^ (q % 8))
    return tp // 2, tp % 2, tq // 4, tq % 4


def place():
    p, q = lax.axis_index("prow"), lax.axis_index("pcol")
    return p // 2, p % 2, q // 4, q % 4


def split(value):
    high = value.astype(BF16)
    return high, (value - high.astype(F32)).astype(BF16)


def dot3(lh, ll, rh, rl):
    total = jnp.dot(lh, rh, preferred_element_type=F32)
    total += jnp.dot(ll, rh, preferred_element_type=F32)
    total += jnp.dot(lh, rl, preferred_element_type=F32)
    return total


def dot6(left, right):
    return jnp.dot(left, right, precision=lax.Precision.HIGHEST, preferred_element_type=F32)


def tdot6(left, right):
    return lax.dot_general(
        left, right, (((0,), (0,)), ((), ())), precision=lax.Precision.HIGHEST, preferred_element_type=F32
    )


def call(kernel, inputs, outputs, limit, flops=0, size=0, scratch=(), specs=None):
    if specs:
        inputs = [
            pltpu.with_memory_space_constraint(value, pltpu.HBM) if spec is HBM else value
            for value, spec in zip(inputs, specs)
        ]
    return pl.pallas_call(
        kernel,
        in_specs=specs or [VMEM] * len(inputs),
        out_specs=[VMEM] * len(outputs),
        out_shape=list(outputs),
        scratch_shapes=list(scratch),
        compiler_params=pltpu.CompilerParams(vmem_limit_bytes=limit << 20),
        cost_estimate=pl.CostEstimate(flops=flops, bytes_accessed=size, transcendentals=0),
        name=(kernel.func if isinstance(kernel, functools.partial) else kernel).__name__,
    )(*inputs)


def kept(*shape):
    return pltpu.VMEM(shape, F32)


def free(*shape):
    return jax.ShapeDtypeStruct(shape, F32)


def split_tiles(rows_ref, _, keep_ref, send_ref):
    high = place()[2] // 2
    for v in range(TPC):
        keep_ref[v] = rows_ref[2 * v + high]
        send_ref[v] = rows_ref[2 * v + 1 - high]


def join_group(own_ref, up_ref, down_ref, far_ref, _, first_ref, second_ref):
    def ordered(ref):
        return jnp.swapaxes(ref[...], 0, 1).reshape(PIECE, NB)

    first_ref[:PIECE] = ordered(own_ref)
    first_ref[PIECE:] = ordered(up_ref)
    second_ref[:PIECE] = ordered(down_ref)
    second_ref[PIECE:] = ordered(far_ref)


def fetch(step, s_ref, held_ref, sem):
    _, c, z, y = place()
    copies = []
    for i, offset in enumerate((0, 3, 1, 2)):
        zz = jnp.where(c == 0, z + step, z + offset) % 4
        yy = jnp.where(c == 0, y + offset, y + step) % 4
        copy = pltpu.make_async_copy(
            s_ref.at[pl.ds((zz * 4 + yy) * SLAB, SLAB), :],
            held_ref.at[pl.ds(i * SLAB, SLAB), :],
            sem.at[i],
        )
        copy.start()
        copies.append(copy)
    return copies


def grids():
    row = lax.broadcasted_iota(jnp.int32, (NB, NB), 0)
    col = lax.broadcasted_iota(jnp.int32, (NB, NB), 1)
    return row, col


def invert_blocks(
    s_ref, l_ref, lbar_ref, own_ref, mine_ref,
    first_s, second_s, strict_ref, inverse_ref, l_out, lbar_out, own_out, mine_out, sem, small,
):
    panel = pltpu.make_async_copy(l_ref, l_out, small.at[0])
    panel.start()
    copies = fetch(0, s_ref, first_s, sem.at[0])
    for i, (src, dst) in enumerate(((lbar_ref, lbar_out), (own_ref, own_out), (mine_ref, mine_out))):
        copy = pltpu.make_async_copy(src, dst, small.at[i + 1])
        copy.start()
        copies.append(copy)
    copies += fetch(3, s_ref, second_s, sem.at[1])
    panel.wait()
    row, col = grids()
    lower = l_out[...]
    by_row = 1.0 / jnp.sum(jnp.where(row == col, lower, 0.0), axis=1, keepdims=True)
    strict = jnp.where(row > col, lower * by_row, 0.0)
    power = jnp.where(row // 16 == col // 16, -strict, 0.0)
    inverse = jnp.where(row == col, 1.0, 0.0) + power
    for _ in range(3):
        power = dot6(power, power)
        inverse = inverse + dot6(power, inverse)
    strict_ref[...] = strict
    inverse_ref[...] = inverse
    for copy in copies:
        copy.wait()


def invert_rest(strict_ref, blocks_ref, l_ref, _, inverse_ref):
    n = NB // 2
    row = lax.broadcasted_iota(jnp.int32, (n, n), 0)
    col = lax.broadcasted_iota(jnp.int32, (n, n), 1)
    strict = [strict_ref[:n, :n], strict_ref[n:, n:]]
    inverse = [blocks_ref[:n, :n], blocks_ref[n:, n:]]
    size = 16
    while size < n:
        beside = (row // (2 * size) == col // (2 * size)) & (row // size != col // size)
        inner = [dot6(jnp.where(beside, strict[i], 0.0), inverse[i]) for i in range(2)]
        inverse = [inverse[i] - dot6(inverse[i], inner[i]) for i in range(2)]
        size *= 2
    below = -dot6(inverse[1], dot6(strict_ref[n:, :n], inverse[0]))
    diagonal = [jnp.where(row == col, l_ref[at : at + n, at : at + n], 0.0) for at in (0, n)]
    by_col = [1.0 / jnp.sum(value, axis=0, keepdims=True) for value in diagonal]
    inverse_ref[:n, :n] = inverse[0] * by_col[0]
    inverse_ref[:n, n:] = jnp.zeros((n, n), F32)
    inverse_ref[n:, :n] = below * by_col[0]
    inverse_ref[n:, n:] = inverse[1] * by_col[1]


def product(lh, ll, s_ref, j):
    at = range(4 * j, 4 * j + 4)
    lines = jnp.concatenate([s_ref[pl.ds(k, GROUP, stride=2 * TPC), :] for k in at], axis=1)
    return dot3(lh, ll, *split(lines))


def beside_copies(copies, compute):
    pl.when(place()[0] >= 0)(compute)
    for copy in copies:
        copy.wait()


def parts(first_ref, second_ref):
    return split(jnp.concatenate([first_ref[...], second_ref[...]], axis=0).T)


def multiply_first(la_ref, lb_ref, s_ref, s_all_ref, out_ref, next_ref, sem):
    def compute():
        lh, ll = parts(la_ref, lb_ref)
        for j in range(3):
            out_ref[:, j * 512 : (j + 1) * 512] = product(lh, ll, s_ref, j)

    beside_copies(fetch(1, s_all_ref, next_ref, sem), compute)


def multiply_up(la_ref, lb_ref, s_ref, acc_ref, s_all_ref, out_ref, next_ref, sem):
    def compute():
        lh, ll = parts(la_ref, lb_ref)
        for j in range(3):
            at = slice(j * 512, (j + 1) * 512)
            out_ref[:, at] = acc_ref[:, at] + product(lh, ll, s_ref, j)

    beside_copies(fetch(2, s_all_ref, next_ref, sem), compute)


def multiply_down(la_ref, lb_ref, s_ref, acc_ref, _, out_ref):
    lh, ll = parts(la_ref, lb_ref)
    for j in range(3):
        at = slice(j * 512, (j + 1) * 512)
        out_ref[:, at] = acc_ref[:, at] + product(lh, ll, s_ref, j)


def multiply_last(la_ref, lb_ref, s_ref, acc_ref, keep_ref, send_ref):
    x, c, z, y = place()
    lh, ll = parts(la_ref, lb_ref)
    turn = 2 * (z % 2) + y // 2
    for j in range(3):
        at = slice(j * 512, (j + 1) * 512)
        part = acc_ref[:, at] + product(lh, ll, s_ref, j)
        turned = part.T.reshape(2, 2, 8, 16, NB)
        for odd in range(2):

            @pl.when((c ^ (y % 2)) == odd)
            def _():
                for i in range(4):
                    away = i ^ turn ^ x
                    near = jnp.where(away == 0, 0, jnp.where(away == 1, 2, jnp.where(away == 3, 1, 3)))
                    far = jnp.where(away == 0, 0, jnp.where(away == 1, 1, jnp.where(away == 3, 2, 3)))
                    mine = jnp.where(c == 0, near, far)
                    other = jnp.where(c == 0, far, near)
                    for v in range(2):
                        keep_ref[mine, 2 * j + v] = turned[v, :, 2 * i + odd]
                        send_ref[other, 2 * j + v] = turned[v, :, 2 * i + 1 - odd]


def add_cores(rows, rows_in, keep_ref, send_ref):
    keep_ref[...] = rows[:2] + rows_in[:2]
    send_ref[...] = rows[2:] + rows_in[2:]


def add_pairs(rows, rows_in, _, __, keep_ref, send_ref):
    keep_ref[...] = rows[0] + rows_in[0]
    send_ref[...] = rows[1] + rows_in[1]


def add_rows(rows, rows_in, keep_ref, send_ref):
    high = place()[2] // 2
    keep_ref[...] = rows[:, high] + rows_in[:, high]
    send_ref[...] = rows[:, 1 - high] + rows_in[:, 1 - high]


def join_rows(keep_ref, other_ref, out_ref):
    high = place()[2] // 2
    for v in range(TPC):
        out_ref[2 * v + high] = keep_ref[v]
        out_ref[2 * v + 1 - high] = other_ref[v]


def finish_rows(own_ref, product_ref, inv_ref, out_ref):
    adjusted = own_ref[...] - 2.0 * product_ref[...]
    out_ref[...] = dot6(adjusted.reshape(PIECE, NB), inv_ref[...]).reshape(UR, 16, NB)


def start_panel(share, own_ref, mine_ref, inv_ref, lbar_ref, l_ref, out_ref, inv_t_ref, l_t_ref):
    row, col = grids()
    inv_t = inv_ref[...].T
    inv_t_ref[...] = inv_t
    l_t_ref[...] = l_ref[...].T
    gram = dot6(inv_t, tdot6(own_ref[...].reshape(PIECE, NB), mine_ref[...].reshape(PIECE, NB)))
    out_ref[...] = lbar_ref[...] * share - jnp.where(row >= col, gram, 0.0)


def finish_panel(
    first_ref, second_ref, l_first_ref, l_second_ref, l_t_ref, inv_t_ref, inv_ref, base_ref, keep_ref, send_ref, second_out
):
    c = place()[1]
    row, col = grids()
    half = PIECE // 2
    cross = tdot6(first_ref[...].reshape(half, NB), l_first_ref[...].reshape(half, NB))
    cross += tdot6(second_ref[...].reshape(half, NB), l_second_ref[...].reshape(half, NB))
    inverse = inv_ref[...]
    inv_t = inv_t_ref[...]
    fresh = base_ref[...] + jnp.where(row >= col, 2.0 * dot6(inv_t, cross), 0.0)
    phi = dot6(l_t_ref[...], fresh)
    phi = jnp.where(row > col, phi, jnp.where(row == col, 0.5 * phi, 0.0))
    full = dot6(dot6(inv_t, phi), inverse)
    result = 0.5 * (full + full.T)
    n = NB // 2
    row, col = row[:n, :n], col[:n, :n]
    last = result[n:, n:]
    mixed = jnp.where(row >= col, result[:n, :n], last)
    diagonal = jnp.sum(jnp.where(row == col, last, 0.0), axis=0, keepdims=True)
    lower = result[n:, :n]
    keep_ref[:n] = jnp.where(c == 0, lower, mixed)
    send_ref[:n] = jnp.where(c == 0, mixed, lower)
    keep_ref[n:] = jnp.broadcast_to(diagonal, (8, n))
    send_ref[n:] = jnp.broadcast_to(diagonal, (8, n))
    second_out[...] = second_ref[...]


def add_two(part, other, out_ref):
    out_ref[...] = part[...] + other[...]


def add_four(part, beyond, near, opposite, _, out_ref):
    out_ref[...] = (part[...] + near[...]) + (beyond[...] + opposite[...])


def unpack(part, rest, out_ref):
    c = place()[1]
    n = NB // 2
    row = lax.broadcasted_iota(jnp.int32, (n, n), 0)
    col = lax.broadcasted_iota(jnp.int32, (n, n), 1)
    lower = jnp.where(c == 0, part[:n], rest[:n])
    mixed = jnp.where(c == 0, rest[:n], part[:n])
    diagonal = jnp.where(c == 0, rest[n : n + 1], part[n : n + 1])
    turned = mixed.T
    out_ref[:n, :n] = jnp.where(row >= col, mixed, turned)
    out_ref[n:, n:] = jnp.where(row == col, diagonal, jnp.where(row < col, mixed, turned))
    out_ref[n:, :n] = lower
    out_ref[:n, n:] = lower.T


def shards(l_panel, l_rows, lbar_panel, lbar_rows, sbar):
    share = 1.0 / (lax.axis_size("prow") * lax.axis_size("pcol"))
    s_lines = sbar.reshape(16 * SLAB, 128)
    mine = jnp.transpose(l_rows[0], (1, 0, 2))
    own = jnp.transpose(lbar_rows[0], (1, 0, 2))
    dma = pltpu.SemaphoreType.DMA
    lines = kept(4 * SLAB + 16, 128)
    square = kept(NB, NB)

    far = permute(mine, first_axis(2))
    up = permute(mine, first_axis(1))
    down = permute(mine, first_axis(-1))
    s0, s3, strict, blocks, l_kept, lbar_kept, own_kept, mine_kept = call(
        invert_blocks,
        [s_lines, l_panel, lbar_panel, own, mine],
        [lines, lines, square, square, square, square, kept(UR, 16, NB), kept(UR, 16, NB)],
        4,
        flops=6 * 12 * NB**3,
        size=10_000_000,
        scratch=[dma((2, 4)), dma((4,))],
        specs=[HBM] * 5,
    )
    tile = kept(TPC, 16, NB)
    rows = permute(mine, to_tiles)
    first, second = call(
        join_group,
        [mine_kept, up, down, far, blocks],
        [free(GROUP // 2, NB)] * 2,
        4,
        size=1_600_000,
        specs=[VMEM] * 4 + [ANY],
    )
    up_first = permute(first, second_axis(1))
    down_second = permute(second, second_axis(-1))
    up_second = permute(second, second_axis(1))
    down_first = permute(first, second_axis(-1))
    far_first = permute(up_first, second_axis(1))
    far_second = permute(down_second, second_axis(-1))
    work = dict(flops=6 * GROUP * COLS * NB, size=6_000_000)
    wide = kept(NB, COLS)
    total, s1 = call(
        multiply_first,
        [first, second, s0, s_lines],
        [wide, lines],
        8,
        scratch=[dma((4,))],
        specs=[VMEM] * 3 + [HBM],
        **work,
    )
    l_keep, l_send = call(split_tiles, [rows, total], [tile, tile], 4, size=800_000, specs=[VMEM, ANY])
    l_other = permute(l_send, opposite_half)
    total, s2 = call(
        multiply_up,
        [up_first, up_second, s3, total, s_lines],
        [wide, lines],
        8,
        scratch=[dma((4,))],
        specs=[VMEM] * 4 + [HBM],
        **work,
    )
    (total,) = call(
        multiply_down,
        [down_first, down_second, s1, total, rows],
        [wide],
        8,
        specs=[VMEM] * 4 + [ANY],
        **work,
    )
    share4 = kept(4, TPC, 2, 16, NB)
    keep, send = call(multiply_last, [far_first, far_second, s2, total], [share4, share4], 8, **work)

    share2 = kept(2, TPC, 2, 16, NB)
    share1 = kept(TPC, 2, 16, NB)
    keep, send = call(add_cores, [keep, permute(send, other_core)], [share2, share2], 6, size=2_000_000)
    (inverse,) = call(
        invert_rest,
        [strict, blocks, l_kept, keep],
        [square],
        6,
        flops=8 * 12 * NB**3,
        size=6_000_000,
        specs=[VMEM] * 3 + [ANY],
    )
    keep, send = call(
        add_pairs,
        [keep, permute(send, halving(0)), inverse, l_other],
        [share1, share1],
        6,
        size=1_000_000,
        specs=[VMEM] * 2 + [ANY] * 2,
    )
    base, inv_t, l_t = call(
        functools.partial(start_panel, share), [own_kept, mine_kept, inverse, lbar_kept, l_kept], [square] * 3, 6,
        flops=2 * 12 * NB**3, size=4_000_000,
    )
    keep, send = call(add_rows, [keep, permute(send, halving(1))], [tile, tile], 6, size=1_000_000)
    half = kept(NB // 2 + 8, NB // 2)
    part, other, send = call(
        finish_panel,
        [keep, send, l_keep, l_other, l_t, inv_t, inverse, base],
        [half, half, tile],
        8,
        flops=6 * 12 * NB**3,
        size=4_000_000,
    )

    (rows,) = call(join_rows, [keep, permute(send, opposite_half)], [free(UR, 16, NB)], 4, size=800_000)
    (part,) = call(add_two, [part, permute(other, other_core)], [half], 4, size=500_000)

    def add_around(stage, after):
        others = [permute(part, crossing(stage, mask)) for mask in (2, 1, 3)]
        return call(add_four, [part, *others, after], [half], 4, size=1_000_000, specs=[VMEM] * 4 + [ANY])

    (part,) = add_around(0, rows)
    rows = permute(rows, to_rows)
    (part,) = add_around(1, inverse)
    (part,) = add_around(2, inverse)
    (abar,) = call(
        finish_rows,
        [own_kept, rows, inverse],
        [free(UR, 16, NB)],
        6,
        flops=12 * PIECE * NB * NB,
        size=1_000_000,
    )
    rest = permute(part, other_core)
    (abar_panel,) = call(unpack, [part, rest], [free(NB, NB)], 4, size=500_000)
    return jnp.transpose(abar, (1, 0, 2))[None], abar_panel


def solution(mesh):
    return jax.shard_map(
        shards,
        mesh=mesh,
        in_specs=(
            P(),
            P("prow", "pcol", None, None),
            P(),
            P("prow", "pcol", None, None),
            P("prow", None, None, "pcol", None, None),
        ),
        out_specs=(P("prow", "pcol", None, None), P()),
        check_vma=False,
    )
```
